32 devices in a mesh: group: 2 (over x), layer: 8 (over z, y), latent: 2 (over core).
Axes of the slice: x: 2, y: 2, z: 4, core: 2. Of those that a mesh axis runs over, the one named last changes fastest.
Arguments:
- residual_in: bfloat16 [2, 2048, 1792], P(None, 'group'), parts along dimension 1, may hold values from -3 to 3
- mlp_target: bfloat16 [2, 2048, 1792], P(None, 'group'), parts along dimension 1, may hold values from -6 to 6
- enc_weight: bfloat16 [2, 1792, 8192], P(None, None, ('layer', 'latent')), may hold values from -0.046875 to 0.046875
- enc_bias: float32 [2, 8192], P(None, ('layer', 'latent')), may hold values from -1 to 1
- dec_weight: bfloat16 [3, 8192, 1792], P(None, ('layer', 'latent')), may hold values from -0.0625 to 0.0625
Outputs:
- grad_enc_weight: bfloat16 [4, 1792, 8192], P('group', None, ('layer', 'latent')), parts along dimension 0
- grad_enc_bias: float32 [4, 8192], P('group', ('layer', 'latent')), parts along dimension 0
- grad_dec_weight: bfloat16 [6, 8192, 1792], P('group', ('layer', 'latent')), parts along dimension 0
The draws below stay inside these ranges and needn't reach their ends.
There are 2 independent parts, one for each index of `group`. The reference program is written for one: setup_inputs(seed, part) draws one part's arguments, and reference() takes and returns one part's arrays. A program takes and returns all parts, laid end to end along the dimension named above; an argument that names none is the same for every part. Nothing has to cross between parts.
All inputs are finite; a program needn't handle non-finite values.
Results may differ from the reference program's by a relative error of at most 0.0059.
Values may be sent and summed in bfloat16 or wider, within the bound.
A program may use at most 128 MiB of HBM per device.

```python
import jax
import jax.numpy as jnp
from jax import lax

D = 1792
FEATURES = 8192
LAYERS = 2
TOK = 1024
PAIRS = 3


def draw_residual_in(key, part):
    key = jax.random.fold_in(key, 11)
    levels = jax.random.randint(key, (LAYERS, TOK, D), -48, 49).astype(jnp.float32)
    return (levels / 32.0).astype(jnp.bfloat16)


def draw_enc_weight(key, part):
    key = jax.random.fold_in(key, 23)
    levels = jax.random.randint(key, (LAYERS, D, FEATURES), -12, 13).astype(jnp.float32)
    return (levels / 256.0).astype(jnp.bfloat16)


def draw_enc_bias(key, part):
    key = jax.random.fold_in(key, 37)
    levels = jax.random.randint(key, (LAYERS, FEATURES), -512, 513).astype(jnp.float32)
    return levels / 512.0


def block_scale(key, extent, shards, low, largest):
    loudness, own = 1.0, jax.random.fold_in(key, 6)
    for position, shards_of in shards:
        steps = jnp.exp(jax.random.uniform(jax.random.fold_in(own, position), (shards_of,), jnp.float32, low / len(shards), largest / len(shards)))
        loudness = loudness * jnp.repeat(steps, extent[position] // shards_of).reshape([-1 if axis == position else 1 for axis in range(len(extent))])
    return loudness


def scatter_about(key, dims, spread, most, cuts=(), dtype=jnp.bfloat16):
    result = jax.random.normal(key, dims, jnp.float32) * spread
    if len(cuts) > 0:
        result = block_scale(key, dims, cuts, -0.22, 0.18) * result
    return jnp.clip(result, min=-most, max=most).astype(dtype)


def setup_inputs(seed: int = 0, part: int = 0) -> dict:
    key_list = jax.random.split(jax.random.key(seed), 6)
    own_keys = jax.random.split(jax.random.fold_in(key_list[5], part), 6)
    return {
        "residual_in": draw_residual_in(jax.random.fold_in(jax.random.fold_in(key_list[5], part), 71), part),
        "mlp_target": scatter_about(own_keys[1], (LAYERS, TOK, D), 1.0, 6.0),
        "enc_weight": draw_enc_weight(jax.random.fold_in(key_list[5], 71), part),
        "enc_bias": draw_enc_bias(jax.random.fold_in(key_list[5], 71), part),
        "dec_weight": scatter_about(key_list[4], (PAIRS, FEATURES, D), FEATURES ** -0.5, 0.0625, ((1, 16),)),
    }


def pair_index(source, target):
    return target * (target + 1) // 2 + source


def reference(residual_in, mlp_target, enc_weight, enc_bias, dec_weight):
    resid_float = residual_in.astype(jnp.float32)
    pre_act = jnp.einsum("ltd,ldf->ltf", resid_float, enc_weight.astype(jnp.float32)) + enc_bias[:, None, :]
    activity = jnp.maximum(pre_act, 0.0).astype(jnp.bfloat16)
    activity = lax.optimization_barrier(activity)
    act_float = activity.astype(jnp.float32)
    dec_float = dec_weight.astype(jnp.float32)
    rebuilt_list = []
    for target in range(LAYERS):
        total = jnp.zeros((TOK, D), jnp.float32)
        for source in range(target + 1):
            total = total + jnp.dot(act_float[source], dec_float[pair_index(source, target)], preferred_element_type=jnp.float32)
        rebuilt_list.append(total)
    rebuilt = jnp.stack(rebuilt_list)
    err_scale = float(TOK) ** -0.5
    error_rows = ((rebuilt - mlp_target.astype(jnp.float32)) * err_scale).astype(jnp.bfloat16)
    error_rows = lax.optimization_barrier(error_rows)
    error_float = error_rows.astype(jnp.float32)
    dec_grads = []
    for target in range(LAYERS):
        for source in range(target + 1):
            block = jnp.dot(act_float[source].T, error_float[target], preferred_element_type=jnp.float32)
            dec_grads.append(block.astype(jnp.bfloat16))
    grad_dec_weight = jnp.stack(dec_grads)
    act_grads = []
    for source in range(LAYERS):
        total = jnp.zeros((TOK, FEATURES), jnp.float32)
        for target in range(source, LAYERS):
            total = total + jnp.dot(error_float[target], dec_float[pair_index(source, target)].T, preferred_element_type=jnp.float32)
        act_grads.append(total)
    grad_act = jnp.stack(act_grads)
    grad_pre = jnp.where(pre_act > 0.0, grad_act, jnp.zeros_like(grad_act))
    grad_enc_bias = jnp.sum(grad_pre, axis=1)
    grad_rounded = grad_pre.astype(jnp.bfloat16)
    grad_rounded = lax.optimization_barrier(grad_rounded)
    grad_enc_weight = jnp.einsum("ltd,ltf->ldf", resid_float, grad_rounded.astype(jnp.float32)).astype(jnp.bfloat16)
    return grad_enc_weight, grad_enc_bias, grad_dec_weight
```

```python
import functools

import jax
import jax.numpy as jnp
from jax import lax
from jax.experimental import pallas as pl
from jax.experimental.pallas import tpu as pltpu
from jax.sharding import PartitionSpec as P

MESH = pl.DeviceIdType.MESH


def pair_index(source, target):
    return target * (target + 1) // 2 + source


def ring_place(index, ring, folded):
    if not folded:
        return index
    side, along = index % 2, index // 2
    return (1 - side) * along + side * (ring - 1 - along)


def ring_index(place, ring, folded):
    if not folded:
        return place
    side = place // (ring // 2)
    return (1 - side) * (2 * place) + side * (2 * (ring - 1 - place) + 1)


def exchange_kernel(
    ring, folded, scale,
    act_ref, dec_ref, target_ref, err_ref,
    part, pair_send, pair_recv, run_send, run_recv, target_own,
    target_sem, pair_sems, run_sems, gather_sems, share_sems,
):
    layers, _, cores, rows, width = part.shape
    half = ring // 2
    core = lax.axis_index("latent")
    other = 1 - core
    me = ring_place(lax.axis_index("layer"), ring, folded)

    def place(distance):
        return (me + distance + ring) % ring

    neighbour = {step: {"layer": ring_index(place(step), ring, folded)} for step in (1, -1)}
    sibling = {"latent": other}

    target_load = pltpu.make_async_copy(
        target_ref.at[:, me, core], target_own, target_sem
    )
    target_load.start()

    barrier = pltpu.get_barrier_semaphore()
    for device in (neighbour[1], neighbour[-1], sibling):
        pl.semaphore_signal(barrier, inc=1, device_id=device, device_id_type=MESH)
    pl.semaphore_wait(barrier, 3)

    chains = [(0, 1, half), (1, -1, half), (0, -1, half - 1), (1, 1, half - 1)]

    def pair_copy(q):
        return pltpu.make_async_remote_copy(
            src_ref=pair_send.at[:, q], dst_ref=pair_recv.at[:, q],
            send_sem=pair_sems.at[0, q], recv_sem=pair_sems.at[1, q],
            device_id=sibling, device_id_type=MESH,
        )

    def run_copy(chain, step):
        return pltpu.make_async_remote_copy(
            src_ref=run_send.at[chain, step], dst_ref=run_recv.at[chain, step],
            send_sem=run_sems.at[0, chain, step], recv_sem=run_sems.at[1, chain, step],
            device_id=neighbour[chains[chain][1]], device_id_type=MESH,
        )

    def gather_copy(chain, step):
        layer, direction, _ = chains[chain]
        block = err_ref.at[layer, place(-direction * step), core]
        return pltpu.make_async_remote_copy(
            src_ref=block, dst_ref=block,
            send_sem=gather_sems.at[0, chain, step], recv_sem=gather_sems.at[1, chain, step],
            device_id=neighbour[direction], device_id_type=MESH,
        )

    def share_copy(layer, q, sender):
        block = err_ref.at[layer, q, sender]
        return pltpu.make_async_remote_copy(
            src_ref=block, dst_ref=block,
            send_sem=share_sems.at[0, layer, q], recv_sem=share_sems.at[1, layer, q],
            device_id=sibling, device_id_type=MESH,
        )

    def decode(order, carry):
        away = half - (order + 1) // 2
        q = place(away * (2 * (order % 2) - 1))
        start = pl.multiple_of(q * (cores * rows), cores * rows)
        for target in range(layers):
            total = jnp.dot(
                act_ref[0, pl.ds(start, cores * rows), :],
                dec_ref[pair_index(0, target)], preferred_element_type=jnp.float32,
            )
            for source in range(1, target + 1):
                total = total + jnp.dot(
                    act_ref[source, pl.ds(start, cores * rows), :],
                    dec_ref[pair_index(source, target)], preferred_element_type=jnp.float32,
                )
            for k in range(cores):
                part[target, q, k] = total[k * rows:(k + 1) * rows]
            pair_send[target, q] = part[target, q, other].astype(jnp.bfloat16)
        pair_copy(q).start()
        return carry

    def own_sum(layer, q):
        return part[layer, q, core] + pair_recv[layer, q].astype(jnp.float32)

    lax.fori_loop(0, 3, decode, 0)
    for step in range(half):
        for away in {0: (half, half - 1, 1 - half)}.get(
            step, (half - 1 - step, step + 1 - half) if step < half - 1 else (0,)
        ):
            pair_copy(place(away)).wait_recv()
        for chain, (layer, direction, hops) in enumerate(chains):
            if step >= hops:
                continue
            value = own_sum(layer, place(direction * (hops - step)))
            if step > 0:
                run_copy(chain, step - 1).wait_recv()
                value = value + run_recv[chain, step - 1].astype(jnp.float32)
            run_send[chain, step] = value.astype(jnp.bfloat16)
            run_copy(chain, step).start()
        if step == 0:
            lax.fori_loop(3, ring, decode, 0)

    target_load.wait()
    for layer in range(layers):
        value = own_sum(layer, me)
        for chain, (of, direction, hops) in sorted(
            enumerate(chains), key=lambda item: item[1][2]
        ):
            if of == layer:
                run_copy(chain, hops - 1).wait_recv()
                value = value + run_recv[chain, hops - 1].astype(jnp.float32)
        error = (value - target_own[layer].astype(jnp.float32)) * scale
        err_ref[layer, me, core] = error.astype(jnp.bfloat16)
        for chain, (of, direction, hops) in enumerate(chains):
            if of == layer:
                gather_copy(chain, 0).start()
        share_copy(layer, me, core).start()

    for step in range(half):
        for chain, (layer, direction, hops) in enumerate(chains):
            if step >= hops:
                continue
            gather_copy(chain, step).wait_recv()
            if step + 1 < hops:
                gather_copy(chain, step + 1).start()
            share_copy(layer, place(-direction * (step + 1)), core).start()

    for chain, (layer, direction, hops) in enumerate(chains):
        for step in range(hops):
            run_copy(chain, step).wait_send()
            gather_copy(chain, step).wait_send()

    def finish(q, carry):
        pair_copy(q).wait_send()
        for layer in range(layers):
            share_copy(layer, q, core).wait_send()
            share_copy(layer, q, other).wait_recv()
        return carry

    lax.fori_loop(0, ring, finish, 0)


def exchange(activity, dec_weight, mlp_target, ring, cores, scale):
    layers, tokens, width = mlp_target.shape
    rows = tokens // (ring * cores)
    half = ring // 2
    blocks = (layers, ring, cores, rows, width)
    err = pl.pallas_call(
        functools.partial(exchange_kernel, ring, ring == 8, scale),
        out_shape=jax.ShapeDtypeStruct(blocks, jnp.bfloat16),
        in_specs=[
            pl.BlockSpec(memory_space=pltpu.VMEM),
            pl.BlockSpec(memory_space=pltpu.VMEM),
            pl.BlockSpec(memory_space=pl.ANY),
        ],
        out_specs=pl.BlockSpec(memory_space=pltpu.VMEM),
        scratch_shapes=[
            pltpu.VMEM(blocks, jnp.float32),
            pltpu.VMEM((layers, ring, rows, width), jnp.bfloat16),
            pltpu.VMEM((layers, ring, rows, width), jnp.bfloat16),
            pltpu.VMEM((4, half, rows, width), jnp.bfloat16),
            pltpu.VMEM((4, half, rows, width), jnp.bfloat16),
            pltpu.VMEM((layers, rows, width), jnp.bfloat16),
            pltpu.SemaphoreType.DMA,
            pltpu.SemaphoreType.DMA((2, ring)),
            pltpu.SemaphoreType.DMA((2, 4, half)),
            pltpu.SemaphoreType.DMA((2, 4, half)),
            pltpu.SemaphoreType.DMA((2, layers, ring)),
        ],
        compiler_params=pltpu.CompilerParams(
            collective_id=0, has_side_effects=True, vmem_limit_bytes=56 * 1024 * 1024
        ),
        cost_estimate=pl.CostEstimate(
            flops=6 * tokens * width * activity.shape[2], bytes_accessed=2 ** 24, transcendentals=0
        ),
    )(activity, dec_weight, mlp_target.reshape(blocks))
    return err.reshape(layers, tokens, width)


def body(ring, cores, residual_in, mlp_target, enc_weight, enc_bias, dec_weight):
    layers = residual_in.shape[0]
    tokens = residual_in.shape[1]
    pre_act = (
        jnp.einsum("ltd,ldf->ltf", residual_in, enc_weight, preferred_element_type=jnp.float32)
        + enc_bias[:, None, :]
    )
    activity = jnp.maximum(pre_act, 0.0).astype(jnp.bfloat16)
    err_scale = float(tokens) ** (-0.5)
    error_all = exchange(activity, dec_weight, mlp_target, ring, cores, err_scale)

    dec_grads = []
    for target in range(layers):
        for source in range(target + 1):
            block = jnp.einsum(
                "tf,td->fd", activity[source], error_all[target], preferred_element_type=jnp.float32
            )
            dec_grads.append(block.astype(jnp.bfloat16))
    grad_dec = jnp.stack(dec_grads)
    act_grads = []
    for source in range(layers):
        total = jnp.einsum(
            "td,fd->tf",
            error_all[source],
            dec_weight[pair_index(source, source)],
            preferred_element_type=jnp.float32,
        )
        for target in range(source + 1, layers):
            total = total + jnp.einsum(
                "td,fd->tf",
                error_all[target],
                dec_weight[pair_index(source, target)],
                preferred_element_type=jnp.float32,
            )
        act_grads.append(total)
    grad_act = jnp.stack(act_grads)
    grad_pre = jnp.where(pre_act > 0.0, grad_act, jnp.zeros_like(grad_act))
    grad_bias = jnp.sum(grad_pre, axis=1)
    grad_rounded = grad_pre.astype(jnp.bfloat16)
    grad_encoder = jnp.einsum(
        "ltd,ltf->ldf", residual_in, grad_rounded, preferred_element_type=jnp.float32
    ).astype(jnp.bfloat16)
    return (grad_encoder, grad_bias, grad_dec)


def solution(mesh):
    placed = (
        P(None, "group", None),
        P(None, "group", None),
        P(None, None, ("layer", "latent")),
        P(None, ("layer", "latent")),
        P(None, ("layer", "latent"), None),
    )
    return jax.shard_map(
        functools.partial(body, mesh.shape["layer"], mesh.shape["latent"]),
        mesh=mesh,
        in_specs=placed,
        out_specs=(
            P("group", None, ("layer", "latent")),
            P("group", ("layer", "latent")),
            P("group", ("layer", "latent"), None),
        ),
        check_vma=False,
    )
```

```python
import functools

import jax
import jax.numpy as jnp
from jax import lax
from jax.experimental import pallas as pl
from jax.experimental.pallas import tpu as pltpu
from jax.sharding import PartitionSpec as P

MESH = pl.DeviceIdType.MESH


def pair_index(source, target):
    return target * (target + 1) // 2 + source


def ring_place(index, ring, folded):
    if not folded:
        return index
    side, along = index % 2, index // 2
    return (1 - side) * along + side * (ring - 1 - along)


def ring_index(place, ring, folded):
    if not folded:
        return place
    side = place // (ring // 2)
    return (1 - side) * (2 * place) + side * (2 * (ring - 1 - place) + 1)


def step_kernel(
    ring, folded, scale,
    resid_hbm, enc_hbm, bias_ref, dec_hbm, target_hbm,
    act_hbm, err_hbm, grad_hbm, bias_grad,
    resid, enc, dec, act, mask, err, grad,
    own_part, pair_send, pair_recv, run_send, run_recv, target_own,
    load_sems, resid_sems, store_sems, pair_sems, run_sems, gather_sems, share_sems,
):
    layers, _, cores, rows, width = err.shape
    half = ring // 2
    core = lax.axis_index("latent")
    other = 1 - core
    me = ring_place(lax.axis_index("layer"), ring, folded)

    def place(distance):
        return (me + distance + ring) % ring

    def in_order(order):
        return place((half - (order + 1) // 2) * (2 * (order % 2) - 1))

    neighbour = {step: {"layer": ring_index(place(step), ring, folded)} for step in (1, -1)}
    sibling = {"latent": other}

    def resid_load(q):
        return pltpu.make_async_copy(resid_hbm.at[:, q], resid.at[:, q], resid_sems.at[q])

    enc_load = pltpu.make_async_copy(enc_hbm, enc, load_sems.at[0])
    dec_load = pltpu.make_async_copy(dec_hbm, dec, load_sems.at[1])
    target_load = pltpu.make_async_copy(
        target_hbm.at[:, me, core], target_own, load_sems.at[2]
    )
    enc_load.start()
    for order in range(3):
        resid_load(in_order(order)).start()
    dec_load.start()
    for order in range(3, ring):
        resid_load(in_order(order)).start()
    target_load.start()

    barrier = pltpu.get_barrier_semaphore()
    for device in (neighbour[1], neighbour[-1], sibling):
        pl.semaphore_signal(barrier, inc=1, device_id=device, device_id_type=MESH)
    pl.semaphore_wait(barrier, 3)

    chains = [(0, 1, half), (1, -1, half), (0, -1, half - 1), (1, 1, half - 1)]

    def pair_copy(q):
        return pltpu.make_async_remote_copy(
            src_ref=pair_send.at[:, q], dst_ref=pair_recv.at[:, q],
            send_sem=pair_sems.at[0, q], recv_sem=pair_sems.at[1, q],
            device_id=sibling, device_id_type=MESH,
        )

    def run_copy(chain, step):
        return pltpu.make_async_remote_copy(
            src_ref=run_send.at[chain, step], dst_ref=run_recv.at[chain, step],
            send_sem=run_sems.at[0, chain, step], recv_sem=run_sems.at[1, chain, step],
            device_id=neighbour[chains[chain][1]], device_id_type=MESH,
        )

    def gather_copy(chain, step):
        layer, direction, _ = chains[chain]
        block = err.at[layer, place(-direction * step), core]
        return pltpu.make_async_remote_copy(
            src_ref=block, dst_ref=block,
            send_sem=gather_sems.at[0, chain, step], recv_sem=gather_sems.at[1, chain, step],
            device_id=neighbour[direction], device_id_type=MESH,
        )

    def share_copy(layer, q, sender):
        block = err.at[layer, q, sender]
        return pltpu.make_async_remote_copy(
            src_ref=block, dst_ref=block,
            send_sem=share_sems.at[0, layer, q], recv_sem=share_sems.at[1, layer, q],
            device_id=sibling, device_id_type=MESH,
        )

    kept = ((act, act_hbm), (err, err_hbm), (grad, grad_hbm))

    def store(i, q):
        here, there = kept[i]
        return pltpu.make_async_copy(here.at[:, q], there.at[:, q], store_sems.at[i, q])

    def encode(order, carry):
        q = in_order(order)
        resid_load(q).wait()
        for layer in range(layers):
            pre = jnp.dot(
                resid[layer, q], enc[layer], preferred_element_type=jnp.float32
            ) + bias_ref[layer]
            act[layer, q] = jnp.maximum(pre, 0.0).astype(jnp.bfloat16)
            mask[layer, q] = jnp.where(pre > 0.0, 1.0, 0.0).astype(jnp.bfloat16)
        store(0, q).start()
        return carry

    def decode(order, carry):
        q = in_order(order)
        for target in range(layers):
            total = jnp.dot(
                act[0, q], dec[pair_index(0, target)], preferred_element_type=jnp.float32
            )
            for source in range(1, target + 1):
                total = total + jnp.dot(
                    act[source, q], dec[pair_index(source, target)],
                    preferred_element_type=jnp.float32,
                )
            own_part[target, q] = jnp.where(core == 0, total[:rows], total[rows:])
            pair_send[target, q] = jnp.where(core == 0, total[rows:], total[:rows]).astype(
                jnp.bfloat16
            )
        pair_copy(q).start()
        return carry

    def own_sum(layer, q):
        return own_part[layer, q] + pair_recv[layer, q].astype(jnp.float32)

    def backward(q):
        for layer in range(layers):
            share_copy(layer, q, other).wait_recv()
        store(1, q).start()
        for source in range(layers):
            total = jnp.zeros((cores * rows, act.shape[3]), jnp.float32)
            for target in range(source, layers):
                total = total + lax.dot_general(
                    err[target, q].reshape(cores * rows, width),
                    dec[pair_index(source, target)],
                    (((1,), (1,)), ((), ())), preferred_element_type=jnp.float32,
                )
            value = jnp.where(mask[source, q].astype(jnp.float32) > 0.0, total, 0.0)
            bias_grad[source] += jnp.sum(value, axis=0, keepdims=True)
            grad[source, q] = value.astype(jnp.bfloat16)
        store(2, q).start()

    enc_load.wait()
    lax.fori_loop(0, 3, encode, 0)
    dec_load.wait()
    lax.fori_loop(0, 3, decode, 0)
    for step in range(half):
        for away in {0: (half, half - 1, 1 - half)}.get(
            step, (half - 1 - step, step + 1 - half) if step < half - 1 else (0,)
        ):
            pair_copy(place(away)).wait_recv()
        for chain, (layer, direction, hops) in enumerate(chains):
            if step >= hops:
                continue
            value = own_sum(layer, place(direction * (hops - step)))
            if step > 0:
                run_copy(chain, step - 1).wait_recv()
                value = value + run_recv[chain, step - 1].astype(jnp.float32)
            run_send[chain, step] = value.astype(jnp.bfloat16)
            run_copy(chain, step).start()
        first, last = 2 * step + 3, min(2 * step + 5, ring)
        if first < last:
            lax.fori_loop(first, last, lambda j, c: decode(j, encode(j, c)), 0)

    target_load.wait()
    bias_grad[...] = jnp.zeros_like(bias_grad)
    for layer in range(layers):
        value = own_sum(layer, me)
        for chain, (of, direction, hops) in sorted(
            enumerate(chains), key=lambda item: item[1][2]
        ):
            if of == layer:
                run_copy(chain, hops - 1).wait_recv()
                value = value + run_recv[chain, hops - 1].astype(jnp.float32)
        error = (value - target_own[layer].astype(jnp.float32)) * scale
        err[layer, me, core] = error.astype(jnp.bfloat16)
        for chain, (of, direction, hops) in enumerate(chains):
            if of == layer:
                gather_copy(chain, 0).start()
        share_copy(layer, me, core).start()

    backward(me)
    for step in range(half):
        for chain, (layer, direction, hops) in enumerate(chains):
            if step >= hops:
                continue
            gather_copy(chain, step).wait_recv()
            if step + 1 < hops:
                gather_copy(chain, step + 1).start()
            share_copy(layer, place(-direction * (step + 1)), core).start()

        def both_sides(side, carry, away=step + 1):
            backward(place(away * (1 - 2 * side)))
            return carry

        lax.fori_loop(0, 2 if step + 1 < half else 1, both_sides, 0)

    for chain, (layer, direction, hops) in enumerate(chains):
        for step in range(hops):
            run_copy(chain, step).wait_send()
            gather_copy(chain, step).wait_send()

    def finish(q, carry):
        pair_copy(q).wait_send()
        for layer in range(layers):
            share_copy(layer, q, core).wait_send()
        for i in range(len(kept)):
            store(i, q).wait()
        return carry

    lax.fori_loop(0, ring, finish, 0)


def step(residual_in, mlp_target, enc_weight, enc_bias, dec_weight, ring, cores, scale):
    layers, tokens, width = mlp_target.shape
    features = enc_weight.shape[2]
    rows = tokens // (ring * cores)
    half = ring // 2
    halves = (layers, ring, cores, rows, width)
    by_width = (layers, ring, cores * rows, width)
    by_feature = (layers, ring, cores * rows, features)
    anywhere = pl.BlockSpec(memory_space=pl.ANY)
    in_vmem = pl.BlockSpec(memory_space=pltpu.VMEM)
    bf16 = jnp.bfloat16
    act, err, grad, bias_grad = pl.pallas_call(
        functools.partial(step_kernel, ring, ring == 8, scale),
        out_shape=(
            jax.ShapeDtypeStruct(by_feature, bf16),
            jax.ShapeDtypeStruct(halves, bf16),
            jax.ShapeDtypeStruct(by_feature, bf16),
            jax.ShapeDtypeStruct((layers, 1, features), jnp.float32),
        ),
        in_specs=[anywhere, anywhere, in_vmem, anywhere, anywhere],
        out_specs=(anywhere, anywhere, anywhere, in_vmem),
        scratch_shapes=[
            pltpu.VMEM(by_width, bf16),
            pltpu.VMEM(enc_weight.shape, bf16),
            pltpu.VMEM(dec_weight.shape, bf16),
            pltpu.VMEM(by_feature, bf16),
            pltpu.VMEM(by_feature, bf16),
            pltpu.VMEM(halves, bf16),
            pltpu.VMEM(by_feature, bf16),
            pltpu.VMEM((layers, ring, rows, width), jnp.float32),
            pltpu.VMEM((layers, ring, rows, width), bf16),
            pltpu.VMEM((layers, ring, rows, width), bf16),
            pltpu.VMEM((4, half, rows, width), bf16),
            pltpu.VMEM((4, half, rows, width), bf16),
            pltpu.VMEM((layers, rows, width), bf16),
            pltpu.SemaphoreType.DMA((3,)),
            pltpu.SemaphoreType.DMA((ring,)),
            pltpu.SemaphoreType.DMA((3, ring)),
            pltpu.SemaphoreType.DMA((2, ring)),
            pltpu.SemaphoreType.DMA((2, 4, half)),
            pltpu.SemaphoreType.DMA((2, 4, half)),
            pltpu.SemaphoreType.DMA((2, layers, ring)),
        ],
        compiler_params=pltpu.CompilerParams(
            collective_id=0, has_side_effects=True, vmem_limit_bytes=60 * 1024 * 1024
        ),
        cost_estimate=pl.CostEstimate(
            flops=16 * tokens * width * features, bytes_accessed=2 ** 25, transcendentals=0
        ),
    )(
        residual_in.reshape(by_width), enc_weight, enc_bias.reshape(layers, 1, features),
        dec_weight, mlp_target.reshape(halves),
    )
    return (
        act.reshape(layers, tokens, features),
        err.reshape(layers, tokens, width),
        grad.reshape(layers, tokens, features),
        bias_grad.reshape(layers, features),
    )


def token_sum_kernel(left_ref, right_ref, out_ref):
    out_ref[0] = lax.dot_general(
        left_ref[0], right_ref[0], (((0,), (0,)), ((), ())),
        preferred_element_type=jnp.float32,
    ).astype(out_ref.dtype)


def token_sum(left, right, pairs, left_of, right_of, cuts):
    _, tokens, rows = left.shape
    width = right.shape[2]
    return pl.pallas_call(
        token_sum_kernel,
        out_shape=jax.ShapeDtypeStruct((pairs, rows, width), jnp.bfloat16),
        grid=(pairs, cuts),
        in_specs=[
            pl.BlockSpec((1, tokens, rows // cuts), lambda p, i: (left_of(p), 0, i)),
            pl.BlockSpec((1, tokens, width), lambda p, i: (right_of(p), 0, 0)),
        ],
        out_specs=pl.BlockSpec((1, rows // cuts, width), lambda p, i: (p, i, 0)),
        compiler_params=pltpu.CompilerParams(vmem_limit_bytes=56 * 1024 * 1024),
        cost_estimate=pl.CostEstimate(
            flops=2 * pairs * tokens * rows * width,
            bytes_accessed=2 * pairs * (tokens * (rows + width) + rows * width),
            transcendentals=0,
        ),
    )(left, right)


def body(ring, cores, residual_in, mlp_target, enc_weight, enc_bias, dec_weight):
    layers, tokens, _ = residual_in.shape
    assert layers == 2 and cores == 2
    act, err, grad, grad_bias = step(
        residual_in, mlp_target, enc_weight, enc_bias, dec_weight,
        ring, cores, float(tokens) ** (-0.5),
    )
    grad_dec = token_sum(act, err, 3, lambda p: p // 2, lambda p: (p + 1) // 2, 1)
    grad_encoder = token_sum(residual_in, grad, 2, lambda p: p, lambda p: p, 2)
    return (grad_encoder, grad_bias, grad_dec)


def solution(mesh):
    placed = (
        P(None, "group", None),
        P(None, "group", None),
        P(None, None, ("layer", "latent")),
        P(None, ("layer", "latent")),
        P(None, ("layer", "latent"), None),
    )
    return jax.shard_map(
        functools.partial(body, mesh.shape["layer"], mesh.shape["latent"]),
        mesh=mesh,
        in_specs=placed,
        out_specs=(
            P("group", None, ("layer", "latent")),
            P("group", ("layer", "latent")),
            P("group", ("layer", "latent"), None),
        ),
        check_vma=False,
    )
```

```python
import functools

import jax
import jax.numpy as jnp
from jax import lax
from jax.experimental import pallas as pl
from jax.experimental.pallas import tpu as pltpu
from jax.sharding import PartitionSpec as P

MESH = pl.DeviceIdType.MESH


def pair_index(source, target):
    return target * (target + 1) // 2 + source


def ring_place(index, ring, folded):
    if not folded:
        return index
    side, along = index % 2, index // 2
    return (1 - side) * along + side * (ring - 1 - along)


def ring_index(place, ring, folded):
    if not folded:
        return place
    side = place // (ring // 2)
    return (1 - side) * (2 * place) + side * (2 * (ring - 1 - place) + 1)


def step_kernel(
    ring, folded, scale,
    resid_hbm, enc_hbm, bias_ref, dec_hbm, target_hbm,
    act_hbm, err_hbm, grad_hbm, bias_grad,
    resid, enc, dec, act, mask, err, grad,
    own_part, pair_send, pair_recv, run_send, run_recv, target_own,
    load_sems, resid_sems, store_sems, pair_sems, run_sems, gather_sems, share_sems,
):
    layers, _, cores, rows, width = err.shape
    half = ring // 2
    core = lax.axis_index("latent")
    other = 1 - core
    me = ring_place(lax.axis_index("layer"), ring, folded)

    def place(distance):
        return (me + distance + ring) % ring

    def in_order(order):
        return place((half - (order + 1) // 2) * (2 * (order % 2) - 1))

    neighbour = {step: {"layer": ring_index(place(step), ring, folded)} for step in (1, -1)}
    sibling = {"latent": other}

    def resid_load(q):
        return pltpu.make_async_copy(resid_hbm.at[:, q], resid.at[:, q], resid_sems.at[q])

    enc_load = pltpu.make_async_copy(enc_hbm, enc, load_sems.at[0])
    dec_load = pltpu.make_async_copy(dec_hbm, dec, load_sems.at[1])
    target_load = pltpu.make_async_copy(
        target_hbm.at[:, me, core], target_own, load_sems.at[2]
    )
    enc_load.start()
    for order in range(3):
        resid_load(in_order(order)).start()
    dec_load.start()
    for order in range(3, ring):
        resid_load(in_order(order)).start()
    target_load.start()

    barrier = pltpu.get_barrier_semaphore()
    for device in (neighbour[1], neighbour[-1], sibling):
        pl.semaphore_signal(barrier, inc=1, device_id=device, device_id_type=MESH)
    pl.semaphore_wait(barrier, 3)

    chains = [(0, 1, half), (1, -1, half), (0, -1, half - 1), (1, 1, half - 1)]

    def pair_copy(q):
        return pltpu.make_async_remote_copy(
            src_ref=pair_send.at[:, q], dst_ref=pair_recv.at[:, q],
            send_sem=pair_sems.at[0, q], recv_sem=pair_sems.at[1, q],
            device_id=sibling, device_id_type=MESH,
        )

    def run_copy(chain, step):
        return pltpu.make_async_remote_copy(
            src_ref=run_send.at[chain, step], dst_ref=run_recv.at[chain, step],
            send_sem=run_sems.at[0, chain, step], recv_sem=run_sems.at[1, chain, step],
            device_id=neighbour[chains[chain][1]], device_id_type=MESH,
        )

    def gather_copy(chain, step):
        layer, direction, _ = chains[chain]
        block = err.at[layer, place(-direction * step), core]
        return pltpu.make_async_remote_copy(
            src_ref=block, dst_ref=block,
            send_sem=gather_sems.at[0, chain, step], recv_sem=gather_sems.at[1, chain, step],
            device_id=neighbour[direction], device_id_type=MESH,
        )

    def share_copy(layer, q, sender):
        block = err.at[layer, q, sender]
        return pltpu.make_async_remote_copy(
            src_ref=block, dst_ref=block,
            send_sem=share_sems.at[0, layer, q], recv_sem=share_sems.at[1, layer, q],
            device_id=sibling, device_id_type=MESH,
        )

    kept = ((act, act_hbm), (err, err_hbm), (grad, grad_hbm))

    def store(i, q):
        here, there = kept[i]
        return pltpu.make_async_copy(here.at[:, q], there.at[:, q], store_sems.at[i, q])

    def encode(order, carry):
        q = in_order(order)
        resid_load(q).wait()
        for layer in range(layers):
            pre = jnp.dot(
                resid[layer, q], enc[layer], preferred_element_type=jnp.float32
            ) + bias_ref[pl.ds(layer, 1), :]
            act[layer, q] = jnp.maximum(pre, 0.0).astype(jnp.bfloat16)
            mask[layer, q] = jnp.where(pre > 0.0, 1.0, 0.0).astype(jnp.bfloat16)
        store(0, q).start()
        return carry

    def decode(order, carry):
        q = in_order(order)
        for target in range(layers):
            total = jnp.dot(
                act[0, q], dec[pair_index(0, target)], preferred_element_type=jnp.float32
            )
            for source in range(1, target + 1):
                total = total + jnp.dot(
                    act[source, q], dec[pair_index(source, target)],
                    preferred_element_type=jnp.float32,
                )
            own_part[target, q] = jnp.where(core == 0, total[:rows], total[rows:])
            pair_send[target, q] = jnp.where(core == 0, total[rows:], total[:rows]).astype(
                jnp.bfloat16
            )
        pair_copy(q).start()
        return carry

    def own_sum(layer, q):
        return own_part[layer, q] + pair_recv[layer, q].astype(jnp.float32)

    def backward(q):
        for layer in range(layers):
            share_copy(layer, q, other).wait_recv()
        store(1, q).start()
        for source in range(layers):
            total = jnp.zeros((cores * rows, act.shape[3]), jnp.float32)
            for target in range(source, layers):
                total = total + lax.dot_general(
                    err[target, q].reshape(cores * rows, width),
                    dec[pair_index(source, target)],
                    (((1,), (1,)), ((), ())), preferred_element_type=jnp.float32,
                )
            value = jnp.where(mask[source, q].astype(jnp.float32) > 0.0, total, 0.0)
            bias_grad[pl.ds(source, 1), :] += jnp.sum(value, axis=0, keepdims=True)
            grad[source, q] = value.astype(jnp.bfloat16)
        store(2, q).start()

    enc_load.wait()
    encode(0, 0)
    dec_load.wait()
    decode(0, 0)
    lax.fori_loop(1, 2, lambda j, c: decode(j, encode(j, c)), 0)
    for step in range(half):
        if step == 0:
            pair_copy(place(half)).wait_recv()
        else:
            for away in (half - 1 - step, step + 1 - half) if step < half - 1 else (0,):
                pair_copy(place(away)).wait_recv()
        for chain, (layer, direction, hops) in enumerate(chains):
            if step >= hops:
                continue
            if step == 0 and chain == 2:
                lax.fori_loop(2, 3, lambda j, c: decode(j, encode(j, c)), 0)
                for away in (half - 1, 1 - half):
                    pair_copy(place(away)).wait_recv()
            value = own_sum(layer, place(direction * (hops - step)))
            if step > 0:
                run_copy(chain, step - 1).wait_recv()
                value = value + run_recv[chain, step - 1].astype(jnp.float32)
            run_send[chain, step] = value.astype(jnp.bfloat16)
            run_copy(chain, step).start()
        first, last = 2 * step + 3, min(2 * step + 5, ring)
        if first < last:
            lax.fori_loop(first, last, lambda j, c: decode(j, encode(j, c)), 0)

    target_load.wait()
    bias_grad[...] = jnp.zeros_like(bias_grad)
    for layer in range(layers):
        value = own_sum(layer, me)
        for chain, (of, direction, hops) in sorted(
            enumerate(chains), key=lambda item: item[1][2]
        ):
            if of == layer:
                run_copy(chain, hops - 1).wait_recv()
                value = value + run_recv[chain, hops - 1].astype(jnp.float32)
        error = (value - target_own[layer].astype(jnp.float32)) * scale
        err[layer, me, core] = error.astype(jnp.bfloat16)
        for chain, (of, direction, hops) in enumerate(chains):
            if of == layer:
                gather_copy(chain, 0).start()
        share_copy(layer, me, core).start()

    backward(me)
    for step in range(half):
        for chain, (layer, direction, hops) in enumerate(chains):
            if step >= hops:
                continue
            gather_copy(chain, step).wait_recv()
            if step + 1 < hops:
                gather_copy(chain, step + 1).start()
            share_copy(layer, place(-direction * (step + 1)), core).start()

        def both_sides(side, carry, away=step + 1):
            backward(place(away * (1 - 2 * side)))
            return carry

        lax.fori_loop(0, 2 if step + 1 < half else 1, both_sides, 0)

    for chain, (layer, direction, hops) in enumerate(chains):
        for step in range(hops):
            run_copy(chain, step).wait_send()
            gather_copy(chain, step).wait_send()

    def finish(q, carry):
        pair_copy(q).wait_send()
        for layer in range(layers):
            share_copy(layer, q, core).wait_send()
        for i in range(len(kept)):
            store(i, q).wait()
        return carry

    lax.fori_loop(0, ring, finish, 0)


def step(residual_in, mlp_target, enc_weight, enc_bias, dec_weight, ring, cores, scale):
    layers, tokens, width = mlp_target.shape
    features = enc_weight.shape[2]
    rows = tokens // (ring * cores)
    half = ring // 2
    halves = (layers, ring, cores, rows, width)
    by_width = (layers, ring, cores * rows, width)
    by_feature = (layers, ring, cores * rows, features)
    anywhere = pl.BlockSpec(memory_space=pl.ANY)
    in_vmem = pl.BlockSpec(memory_space=pltpu.VMEM)
    bf16 = jnp.bfloat16
    act, err, grad, bias_grad = pl.pallas_call(
        functools.partial(step_kernel, ring, ring == 8, scale),
        out_shape=(
            jax.ShapeDtypeStruct(by_feature, bf16),
            jax.ShapeDtypeStruct(halves, bf16),
            jax.ShapeDtypeStruct(by_feature, bf16),
            jax.ShapeDtypeStruct((layers, features), jnp.float32),
        ),
        in_specs=[anywhere, anywhere, in_vmem, anywhere, anywhere],
        out_specs=(anywhere, anywhere, anywhere, in_vmem),
        scratch_shapes=[
            pltpu.VMEM(by_width, bf16),
            pltpu.VMEM(enc_weight.shape, bf16),
            pltpu.VMEM(dec_weight.shape, bf16),
            pltpu.VMEM(by_feature, bf16),
            pltpu.VMEM(by_feature, bf16),
            pltpu.VMEM(halves, bf16),
            pltpu.VMEM(by_feature, bf16),
            pltpu.VMEM((layers, ring, rows, width), jnp.float32),
            pltpu.VMEM((layers, ring, rows, width), bf16),
            pltpu.VMEM((layers, ring, rows, width), bf16),
            pltpu.VMEM((4, half, rows, width), bf16),
            pltpu.VMEM((4, half, rows, width), bf16),
            pltpu.VMEM((layers, rows, width), bf16),
            pltpu.SemaphoreType.DMA((3,)),
            pltpu.SemaphoreType.DMA((ring,)),
            pltpu.SemaphoreType.DMA((3, ring)),
            pltpu.SemaphoreType.DMA((2, ring)),
            pltpu.SemaphoreType.DMA((2, 4, half)),
            pltpu.SemaphoreType.DMA((2, 4, half)),
            pltpu.SemaphoreType.DMA((2, layers, ring)),
        ],
        compiler_params=pltpu.CompilerParams(
            collective_id=0, has_side_effects=True, vmem_limit_bytes=60 * 1024 * 1024
        ),
        cost_estimate=pl.CostEstimate(
            flops=16 * tokens * width * features, bytes_accessed=2 ** 25, transcendentals=0
        ),
    )(
        residual_in.reshape(by_width), enc_weight, enc_bias,
        dec_weight, mlp_target.reshape(halves),
    )
    return (
        act.reshape(layers, tokens, features),
        err.reshape(layers, tokens, width),
        grad.reshape(layers, tokens, features),
        bias_grad,
    )


def token_sum_kernel(left_ref, right_ref, out_ref):
    out_ref[0] = lax.dot_general(
        left_ref[0], right_ref[0], (((0,), (0,)), ((), ())),
        preferred_element_type=jnp.float32,
    ).astype(out_ref.dtype)


def token_sum(left, right, pairs, left_of, right_of, cuts):
    _, tokens, rows = left.shape
    width = right.shape[2]
    return pl.pallas_call(
        token_sum_kernel,
        out_shape=jax.ShapeDtypeStruct((pairs, rows, width), jnp.bfloat16),
        grid=(pairs, cuts),
        in_specs=[
            pl.BlockSpec((1, tokens, rows // cuts), lambda p, i: (left_of(p), 0, i)),
            pl.BlockSpec((1, tokens, width), lambda p, i: (right_of(p), 0, 0)),
        ],
        out_specs=pl.BlockSpec((1, rows // cuts, width), lambda p, i: (p, i, 0)),
        compiler_params=pltpu.CompilerParams(vmem_limit_bytes=56 * 1024 * 1024),
        cost_estimate=pl.CostEstimate(
            flops=2 * pairs * tokens * rows * width,
            bytes_accessed=2 * pairs * (tokens * (rows + width) + rows * width),
            transcendentals=0,
        ),
    )(left, right)


def body(ring, cores, residual_in, mlp_target, enc_weight, enc_bias, dec_weight):
    layers, tokens, _ = residual_in.shape
    assert layers == 2 and cores == 2
    act, err, grad, grad_bias = step(
        residual_in, mlp_target, enc_weight, enc_bias, dec_weight,
        ring, cores, float(tokens) ** (-0.5),
    )
    grad_dec = token_sum(act, err, 3, lambda p: p // 2, lambda p: (p + 1) // 2, 1)
    grad_encoder = token_sum(residual_in, grad, 2, lambda p: p, lambda p: p, 2)
    return (grad_encoder, grad_bias, grad_dec)


def solution(mesh):
    placed = (
        P(None, "group", None),
        P(None, "group", None),
        P(None, None, ("layer", "latent")),
        P(None, ("layer", "latent")),
        P(None, ("layer", "latent"), None),
    )
    return jax.shard_map(
        functools.partial(body, mesh.shape["layer"], mesh.shape["latent"]),
        mesh=mesh,
        in_specs=placed,
        out_specs=(
            P("group", None, ("layer", "latent")),
            P("group", ("layer", "latent")),
            P("group", ("layer", "latent"), None),
        ),
        check_vma=False,
    )
```
